32 devices in a mesh: gx: 2 (over x), gy: 4 (over y, core), row: 4 (over z).
Axes of the slice: x: 2, y: 2, z: 4, core: 2. Of those that a mesh axis runs over, the one named last changes fastest.
Arguments:
- tokens: bfloat16 [4, 896, 1664], P('row', 'gx', 'gy'), may hold values from -6 to 6
- segments: int32 [4, 896], P('row'), may hold values from 0 to 7, never falling along the last dimension, each value on 1 to 672 neighbouring positions
- gain_attn: float32 [1664], replicated, may hold values from 0.1 to 1.9
- w_query: bfloat16 [1664, 1664], P('gx', 'gy'), as said below
- w_key: bfloat16 [1664, 1664], P('gx', 'gy'), as said below
- w_value: bfloat16 [1664, 1664], P('gx', 'gy'), may hold values from -0.15625 to 0.15625
- w_out: bfloat16 [1664, 1664], P('gy'), may hold values from -0.15625 to 0.15625
- gain_mlp: float32 [1664], replicated, may hold values from 0.1 to 1.9
- w_up: bfloat16 [1664, 8192], P('gx', 'gy'), may hold values from -0.15625 to 0.15625
- w_down: bfloat16 [8192, 1664], P('gy', 'gx'), may hold values from -0.0625 to 0.0625
- w_merge: bfloat16 [4, 1664, 1664], P(None, 'gy', 'gx'), may hold values from -0.078125 to 0.078125
- merge_groups: int32 [4, 224, 4], P('row', 'gx'), may hold values from 0 to 447, as said below
- sources: int32 [4, 224], P('row', 'gx'), may hold values from 0 to 447, as said below
Outputs:
- layer_out: bfloat16 [4, 896, 1664], P('row', 'gx', 'gy')
- returned: bfloat16 [4, 224, 1664], P('row', 'gx', 'gy')
The draws below stay inside these ranges and needn't reach their ends.
Inputs may be any that keep to these rules, and one draw needn't show every extreme that they name: `segments`: ids never fall along a row group's tokens; each of the 8 ids holds 1 to 672 tokens, one exactly 672. `merge_groups`: for every row group and every block of 112 merged rows (one index of gx), the four positions of all its groups name each of 0 to 447 exactly once. `sources`: for every block b of 112 merged rows, the values over all row groups at that block name each of 0 to 447 exactly once. `w_query`: a real matrix whose entries lie within -161.2 and 161.2 over the square root of 1664. `w_key`: a real matrix whose entries lie within -4 and 4 over the square root of 1664.
All inputs are finite; a program needn't handle non-finite values.
Results may differ from the reference program's by a relative error of at most 0.029.
Values may be sent and summed in bfloat16 or wider, within the bound.
No kernel may reach another device: no remote copies, remote signals or barrier semaphores. Data moves between devices by JAX's collectives and lax.ppermute only.
A program may use at most 64 MiB of HBM per device.

```python
import math
import jax
import jax.numpy as jnp
import numpy as np
from jax import lax

D = 1664
H = 16
HD = 104
FF = 8192
TOK_DEV = 448
SEQ = 896
MERGE_DEV = 112
MERGED = 224
SEGS = 8
SEG_MOST = 672
N_GX = 2
N_ROW = 4


def truncated(sub_key, shape):
    return jax.random.truncated_normal(sub_key, -4.0, 4.0, shape, jnp.float32)


def key_base(key):
    return truncated(jax.random.fold_in(key, 11), (D, D)) * D ** (-0.5)


def draw_w_key(key, part):
    return key_base(key).astype(jnp.bfloat16)


def draw_w_query(key, part):
    fresh = truncated(jax.random.fold_in(key, 13), (D, D)) * D ** (-0.5)
    return (3.0 * fresh).astype(jnp.bfloat16)


def draw_merge_groups(key, part):
    key_list = jax.random.split(key, N_ROW * N_GX)
    shuffled = jax.vmap(lambda sub_key: jax.random.permutation(sub_key, TOK_DEV))(key_list)
    return shuffled.reshape(N_ROW, MERGED, 4).astype(jnp.int32)


def draw_sources(key, part):
    key_list = jax.random.split(key, N_GX)
    shuffled = jax.vmap(lambda sub_key: jax.random.permutation(sub_key, N_ROW * MERGE_DEV))(key_list)
    shuffled = shuffled.reshape(N_GX, N_ROW, MERGE_DEV).transpose(1, 0, 2)
    return shuffled.reshape(N_ROW, MERGED).astype(jnp.int32)


def level_of(key, shape, pieces, least, largest):
    def one(position, shards_of):
        draws = jax.random.uniform(jax.random.fold_in(jax.random.fold_in(key, 6), position), (shards_of,), jnp.float32, least / len(pieces), largest / len(pieces))
        return jnp.repeat(jnp.exp(draws), shape[position] // shards_of).reshape((-1,) + (1,) * (len(shape) - position - 1))

    level = one(*pieces[0])
    for cut in pieces[1:]:
        level = level * one(*cut)
    return level


def split_up(count, total, reach, skew):
    loads = [(1 << 20) // math.isqrt(standing ** skew) + 1 for standing in range(2, count + 1)]
    rest, given = total - reach - (count - 1), [1] * (count - 1)
    while rest > 0:
        free = [i for i in range(count - 1) if given[i] < reach]
        whole, left = sum([loads[i] for i in free]), rest
        for i in free:
            extra = min(reach - given[i], max(1, left * loads[i] // whole), rest)
            given[i] = given[i] + extra
            rest = rest - extra
    return np.array([reach] + given)


def uneven(rng, amount, total, limit, slope):
    if amount == 2:
        one = jax.random.randint(rng, (), max(1, total - limit), min(limit, total - 1) + 1)
        return jnp.stack([one, total - one])
    lengths = jnp.asarray(split_up(amount, total, limit, slope), jnp.int32)
    couples = (amount - 1) // 2
    giver, taker = lengths[1:1 + 2 * couples:2], lengths[2:2 + 2 * couples:2]
    slack = jnp.minimum(giver - 1, limit - taker)
    passed = jax.random.randint(jax.random.fold_in(rng, 1), (couples,), 0, 1 << 20) % (slack + 1)
    lengths = lengths.at[1:1 + 2 * couples:2].set(giver - passed).at[2:2 + 2 * couples:2].set(taker + passed)
    return lengths[jax.random.permutation(jax.random.fold_in(rng, 2), amount)]


def gaussian(own_key, extent, width, most, pieces=(), kind=jnp.bfloat16):
    entries = jax.random.normal(own_key, extent, jnp.float32) * width
    if len(pieces) > 0:
        entries = level_of(own_key, extent, pieces, -0.22, 0.18) * entries
    return jnp.clip(entries, min=-most, max=most).astype(kind)


def setup_inputs(seed: int = 0) -> dict:
    keys = jax.random.split(jax.random.key(seed), 14)
    return {
        "tokens": gaussian(keys[0], (N_ROW, SEQ, D), 1.0, 6.0, ((0, 4), (1, 2), (2, 4))),
        "segments": jax.vmap(lambda own: jnp.searchsorted(jnp.cumsum(uneven(own, SEGS, SEQ, SEG_MOST, 2)), jnp.arange(SEQ), side="right"))(jax.random.split(keys[1], N_ROW)).reshape((N_ROW, SEQ)).astype(jnp.int32),
        "gain_attn": jnp.clip(1.0 + 0.18 * jax.random.normal(keys[2], (D,), jnp.float32), 0.1, 1.9),
        "w_query": draw_w_query(jax.random.fold_in(keys[13], 71), 0),
        "w_key": draw_w_key(jax.random.fold_in(keys[13], 71), 0),
        "w_value": gaussian(keys[5], (D, D), D ** -0.5, 0.15625, ((0, 2), (1, 4))),
        "w_out": gaussian(keys[6], (D, D), D ** -0.5, 0.15625, ((0, 4),)),
        "gain_mlp": jnp.clip(1.0 + 0.18 * jax.random.normal(keys[7], (D,), jnp.float32), 0.1, 1.9),
        "w_up": gaussian(keys[8], (D, FF), D ** -0.5, 0.15625, ((0, 2), (1, 4))),
        "w_down": gaussian(keys[9], (FF, D), FF ** -0.5, 0.0625, ((0, 4), (1, 2))),
        "w_merge": gaussian(keys[10], (4, D, D), (4 * D) ** -0.5, 0.078125, ((1, 4), (2, 2))),
        "merge_groups": draw_merge_groups(jax.random.fold_in(keys[13], 71), 0),
        "sources": draw_sources(jax.random.fold_in(keys[13], 71), 0),
    }


EPS = 1e-06
NEG = -1e+30

def normalize(tok_rows, gain):
    tok_rows = tok_rows.astype(jnp.float32)
    row_mean = lax.optimization_barrier(jnp.mean(tok_rows, axis=-1, keepdims=True))
    centred = tok_rows - row_mean
    row_var = lax.optimization_barrier(jnp.mean(centred * centred, axis=-1, keepdims=True))
    return (centred * lax.rsqrt(row_var + EPS) * gain.astype(jnp.float32)).astype(jnp.bfloat16)

def reference(tokens, segments, gain_attn, w_query, w_key, w_value, w_out, gain_mlp, w_up, w_down, w_merge, merge_groups, sources):
    scale = HD ** (-0.5)

    def by_head(matrix):
        return matrix.reshape(SEQ, H, HD).transpose(1, 0, 2)

    def one_group(inputs):
        tok_rows, seg_ids = inputs
        normed = normalize(tok_rows, gain_attn)
        queries = jnp.dot(normed, w_query, preferred_element_type=jnp.float32).astype(jnp.bfloat16)
        key_rows = jnp.dot(normed, w_key, preferred_element_type=jnp.float32).astype(jnp.bfloat16)
        value_rows = jnp.dot(normed, w_value, preferred_element_type=jnp.float32).astype(jnp.bfloat16)
        same_seg = seg_ids[:, None] == seg_ids[None, :]

        def one_head(parts):
            q_head, k_head, v_head = parts
            scores = jnp.dot(q_head, k_head.T, preferred_element_type=jnp.float32) * scale
            scores = jnp.where(same_seg, scores, NEG)
            row_top = lax.optimization_barrier(jnp.max(scores, axis=-1, keepdims=True))
            weights = jnp.where(same_seg, jnp.exp(scores - row_top), 0.0)
            row_total = lax.optimization_barrier(jnp.sum(weights, axis=-1, keepdims=True))
            mixed = jnp.dot(weights.astype(jnp.bfloat16), v_head, preferred_element_type=jnp.float32)
            return mixed / row_total
        attended = lax.map(one_head, (by_head(queries), by_head(key_rows), by_head(value_rows)))
        attended = attended.transpose(1, 0, 2).reshape(SEQ, D).astype(jnp.bfloat16)
        after_attn = (tok_rows.astype(jnp.float32) + jnp.dot(attended, w_out, preferred_element_type=jnp.float32)).astype(jnp.bfloat16)
        normed_mlp = normalize(after_attn, gain_mlp)
        hidden = jax.nn.gelu(jnp.dot(normed_mlp, w_up, preferred_element_type=jnp.float32), approximate=False).astype(jnp.bfloat16)
        return (after_attn.astype(jnp.float32) + jnp.dot(hidden, w_down, preferred_element_type=jnp.float32)).astype(jnp.bfloat16)
    layer_out = lax.map(one_group, (tokens, segments))
    block_start = jnp.arange(MERGED, dtype=jnp.int32) // MERGE_DEV * TOK_DEV
    merge_matrix = w_merge.reshape(4 * D, D)

    def merge_group(inputs):
        out_rows, group_ids = inputs
        picked = out_rows[(group_ids + block_start[:, None]).astype(jnp.int32)].reshape(MERGED, 4 * D)
        return jnp.dot(picked, merge_matrix, preferred_element_type=jnp.float32).astype(jnp.bfloat16)
    merged = lax.map(merge_group, (layer_out, merge_groups))
    slot_block = jnp.arange(MERGED, dtype=jnp.int32) // MERGE_DEV
    source_group = (sources // MERGE_DEV).astype(jnp.int32)
    source_row = (slot_block[None, :] * MERGE_DEV + sources % MERGE_DEV).astype(jnp.int32)
    returned = merged[source_group, source_row]
    return (layer_out, returned)
```

```python
import functools

import jax
import jax.numpy as jnp
from jax import lax
from jax.experimental import pallas as pl
from jax.experimental.pallas import tpu as pltpu
from jax.sharding import PartitionSpec as P

HD = 104


EPS = 1e-06
NEG = -1e30
VMEM_LIMIT = 30 * 1024 * 1024
SMALL_LIMIT = 24 * 1024 * 1024
OUT_EARLY = 128
LOG2_E = 1.4426950408889634


def normalize(tok_rows, gain):
    tok_rows = tok_rows.astype(jnp.float32)
    row_mean = jnp.mean(tok_rows, axis=-1, keepdims=True)
    centred = tok_rows - row_mean
    row_var = jnp.mean(centred * centred, axis=-1, keepdims=True)
    return (centred * lax.rsqrt(row_var + EPS) * gain).astype(jnp.bfloat16)


def general_body(
    tokens,
    segments,
    gain_attn,
    w_query,
    w_key,
    w_value,
    w_out,
    gain_mlp,
    w_up,
    w_down,
    w_merge,
    merge_groups,
    sources,
):
    tok_local = tokens[0]
    row_count = tok_local.shape[0]
    seg_all = segments[0]
    col_count = w_query.shape[1]
    head_count = col_count // HD
    scale = HD ** (-0.5)
    gathered = lax.all_gather(tok_local, "gy", axis=1, tiled=True)
    normed = normalize(gathered, gain_attn)
    pieces = (
        lax.all_gather(w_query, "gx", axis=0, tiled=True),
        lax.all_gather(w_key, "gx", axis=0, tiled=True),
        lax.all_gather(w_value, "gx", axis=0, tiled=True),
    )
    feat_part = normed
    q_sum = jnp.dot(feat_part, pieces[0], preferred_element_type=jnp.float32)
    k_sum = jnp.dot(feat_part, pieces[1], preferred_element_type=jnp.float32)
    v_sum = jnp.dot(feat_part, pieces[2], preferred_element_type=jnp.float32)
    queries = q_sum.astype(jnp.bfloat16).reshape(row_count, head_count, HD)
    key_rows = k_sum.astype(jnp.bfloat16)
    value_rows = v_sum.astype(jnp.bfloat16)
    own_seg = lax.dynamic_slice_in_dim(seg_all, lax.axis_index("gx") * row_count, row_count)
    start_state = (
        jnp.full((row_count, head_count), NEG, jnp.float32),
        jnp.zeros((row_count, head_count), jnp.float32),
        jnp.zeros((row_count, head_count, HD), jnp.float32),
    )
    pieces = (
        lax.all_gather(key_rows, "gx", axis=0, tiled=True),
        lax.all_gather(value_rows, "gx", axis=0, tiled=True),
    )
    key_count = pieces[0].shape[0]
    block_len = min(row_count, key_count)
    block_total = key_count // block_len

    def one_block(step, old):
        block_keys = lax.dynamic_slice_in_dim(pieces[0], step * block_len, block_len, 0)
        block_values = lax.dynamic_slice_in_dim(pieces[1], step * block_len, block_len, 0)
        key_seg = lax.dynamic_slice_in_dim(seg_all, step * block_len, block_len)
        row_top, row_total, weighted = old
        key_heads = block_keys.reshape(block_len, head_count, HD)
        value_heads = block_values.reshape(block_len, head_count, HD)
        scores = (
            jnp.einsum("qhd,khd->qhk", queries, key_heads, preferred_element_type=jnp.float32)
            * scale
        )
        same_seg = (own_seg[:, None] == key_seg[None, :])[:, None, :]
        scores = jnp.where(same_seg, scores, NEG)
        new_top = jnp.maximum(row_top, jnp.max(scores, axis=-1))
        weights = jnp.where(same_seg, jnp.exp(scores - new_top[:, :, None]), 0.0)
        rescale = jnp.exp(row_top - new_top)
        row_total = row_total * rescale + jnp.sum(weights, axis=-1)
        weighted = weighted * rescale[:, :, None] + jnp.einsum(
            "qhk,khd->qhd",
            weights.astype(jnp.bfloat16),
            value_heads,
            preferred_element_type=jnp.float32,
        )
        return (new_top, row_total, weighted)

    row_top, row_total, weighted = lax.fori_loop(0, block_total, one_block, start_state)
    attended = (weighted / row_total[:, :, None]).reshape(row_count, col_count).astype(jnp.bfloat16)
    out_cols = lax.all_to_all(w_out, "gy", split_axis=1, concat_axis=0, tiled=True)
    attn_out = jnp.dot(
        lax.all_gather(attended, "gy", axis=1, tiled=True),
        out_cols,
        preferred_element_type=jnp.float32,
    )
    after_attn = (tok_local.astype(jnp.float32) + attn_out).astype(jnp.bfloat16)
    gathered_mlp = lax.all_gather(after_attn, "gy", axis=1, tiled=True)
    normed_mlp = normalize(gathered_mlp, gain_mlp)
    feat_part = normed_mlp
    hidden_sum = jnp.dot(
        feat_part,
        lax.all_gather(w_up, "gx", axis=0, tiled=True),
        preferred_element_type=jnp.float32,
    )
    hidden = jax.nn.gelu(hidden_sum, approximate=False).astype(jnp.bfloat16)
    partials = jnp.dot(
        hidden, lax.all_gather(w_down, "gx", axis=1, tiled=True), preferred_element_type=jnp.float32
    )
    mlp_out = lax.psum_scatter(
        partials.astype(jnp.bfloat16), "gy", scatter_dimension=1, tiled=True
    ).astype(jnp.float32)
    after_mlp = (after_attn.astype(jnp.float32) + mlp_out).astype(jnp.bfloat16)
    picked = after_mlp[merge_groups[0]]
    merge_terms = jnp.einsum(
        "mkc,kcn->mn",
        picked,
        lax.all_gather(w_merge, "gx", axis=2, tiled=True),
        preferred_element_type=jnp.float32,
    )
    merged = lax.psum_scatter(
        merge_terms.astype(jnp.bfloat16), "gy", scatter_dimension=1, tiled=True
    )
    pooled = lax.all_gather(merged[None], "row", axis=0, tiled=True)
    stacked = pooled.reshape(-1, merged.shape[1])
    returned = stacked[sources[0]]
    return (after_mlp[None], returned[None])


def swap_x(arr):
    return lax.ppermute(arr, "gx", [(0, 1), (1, 0)])


def swap_y(arr):
    return lax.ppermute(arr, "gy", [(i, i ^ 2) for i in range(4)])


def swap_core(arr):
    return lax.ppermute(arr, "gy", [(i, i ^ 1) for i in range(4)])


def swap_row(arr, step):
    count = lax.axis_size("row")
    return lax.ppermute(arr, "row", [(i, i ^ step) for i in range(count)])


def gather_eight(own):
    over_x = swap_x(own)
    over_y = swap_y(own)
    held = [own, over_y, over_x, swap_y(over_x)]
    return held + [swap_core(part) for part in held]


PLACES = tuple((dx, dy, dc) for dc in (0, 1) for dx in (0, 1) for dy in (0, 1))


def position():
    gx = lax.axis_index("gx")
    gy = lax.axis_index("gy")
    return gx, gy // 2, gy % 2


def run_copies(pairs, sem):
    copies = [pltpu.make_async_copy(src, dst, sem.at[i]) for i, (src, dst) in enumerate(pairs)]
    for copy in copies:
        copy.start()
    return copies


def token_copies(refs, tok_scr):
    gx, y, core = position()
    width = refs[0].shape[0]
    pairs = []
    for ref, (dx, dy, dc) in zip(refs, PLACES):
        row = pl.multiple_of(((y ^ dy) * 2 + (core ^ dc)) * width, 16)
        pairs.append((ref, tok_scr.at[gx ^ dx, pl.ds(row, width)]))
    return pairs


STEP = 64


def column(row, scratch):
    scratch[...] = jnp.broadcast_to(row, (8, row.shape[1])).T


def side_by_side(pair, at):
    return jnp.concatenate([pair[0, at].astype(jnp.float32), pair[1, at].astype(jnp.float32)], axis=1)


def fold(rows):
    return jnp.sum(rows.reshape(rows.shape[0] // 8, 8, rows.shape[1]), axis=0)


def norm_of(pivot, first, second, feats):
    shift = jnp.sum(first, axis=0, keepdims=True) / feats
    variance = jnp.maximum(jnp.sum(second, axis=0, keepdims=True) / feats - shift * shift, 0.0)
    return pivot + shift, lax.rsqrt(variance + EPS)


def norm_tokens(pair, gain, out):
    _, feats, count = pair.shape
    steps = feats // STEP
    pivots = [pair[g, :16].astype(jnp.float32)[:1] for g in range(2)]

    def add_up(i, totals):
        at = pl.ds(pl.multiple_of(i * STEP, STEP), STEP)
        new = []
        for g in range(2):
            rows = pair[g, at].astype(jnp.float32) - pivots[g]
            new.append(totals[2 * g] + fold(rows))
            new.append(totals[2 * g + 1] + fold(rows * rows))
        return tuple(new)

    zero = jnp.zeros((8, count), jnp.float32)
    totals = lax.fori_loop(0, steps, add_up, (zero,) * 4)
    moments = [norm_of(pivots[g], totals[2 * g], totals[2 * g + 1], feats) for g in range(2)]
    mean, scale = (jnp.concatenate([moments[0][i], moments[1][i]], axis=1) for i in range(2))

    def write(i, carry):
        at = pl.ds(pl.multiple_of(i * STEP, STEP), STEP)
        rows = side_by_side(pair, at) - mean
        out[at, :] = (rows * scale * gain[at, :1]).astype(jnp.bfloat16)
        return carry

    lax.fori_loop(0, steps, write, 0)


def matmul(lhs, rhs):
    return jnp.dot(lhs, rhs, preferred_element_type=jnp.float32)


def dot_first(lhs, rhs):
    return lax.dot_general(lhs, rhs, (((0,), (0,)), ((), ())), preferred_element_type=jnp.float32)


def attention_kernel(*refs):
    shards = refs[:8]
    gain, w_query, w_key, w_value, w_got, w_got_row, w_got_key, segments = refs[8:16]
    out, tok_scr, norm_scr, w_scr, qkv_scr, att_scr, gain_scr, seg_scr, sem = refs[-9:]
    gx, y, core = position()
    plane = lax.axis_index("row") % 2
    cols = out.shape[0]
    pairs = token_copies(shards, tok_scr)
    own = pl.ds(pl.multiple_of(gx * cols, 16), cols)
    for i, ref in enumerate((w_query, w_key, w_value)):
        pairs.append((ref.at[own], w_scr.at[gx, pl.ds(i * cols, cols)]))
    pairs.append((w_got, w_scr.at[1 - gx, pl.ds(pl.multiple_of(2 * cols * plane, 16), cols)]))
    pairs.append((w_got_row, w_scr.at[1 - gx, pl.ds(pl.multiple_of(2 * cols * (1 - plane), 16), cols)]))
    pairs.append((w_got_key, w_scr.at[1 - gx, pl.ds(cols, cols)]))
    copies = run_copies(pairs, sem)
    column(gain[...], gain_scr)
    column(segments[...], seg_scr)
    for copy in copies[:8]:
        copy.wait()
    norm_tokens(tok_scr, gain_scr, norm_scr)
    for copy in copies[8:]:
        copy.wait()
    feats, total = norm_scr.shape
    depth = feats // 2
    qkv_scr[...] = matmul(w_scr[0], norm_scr[:depth]) + matmul(w_scr[1], norm_scr[depth:])
    scale = HD ** (-0.5) * LOG2_E
    for head in range(cols // HD):
        begin = head * HD
        keys = qkv_scr[cols + begin : cols + begin + HD].T.astype(jnp.bfloat16)
        values = qkv_scr[2 * cols + begin : 2 * cols + begin + HD].astype(jnp.bfloat16)
        for start in range(0, total, 256):
            at = slice(start, min(start + 256, total))
            scores = matmul(keys, (qkv_scr[begin : begin + HD, at] * scale).astype(jnp.bfloat16))
            scores = jnp.where(seg_scr[:, :1] == segments[:, at], scores, NEG)
            weights = jnp.exp2(scores - jnp.max(scores, axis=0, keepdims=True))
            row_total = jnp.sum(weights, axis=0, keepdims=True)
            att_scr[begin : begin + HD, at] = matmul(values, weights.astype(jnp.bfloat16)) / row_total
    out[...] = att_scr[...].astype(jnp.bfloat16)


def project_kernel(*refs):
    tokens, attended, weights, gain = refs[:8], refs[8:16], refs[16:22], refs[22]
    normed, own, tok_scr, att_scr, w_scr, aft_scr, gain_scr, sem = refs[-8:]
    gx, y, core = position()
    width = own.shape[0]
    cols = attended[0].shape[0]
    feats, total = att_scr.shape
    pairs = []
    for ref, (dx, dy, dc) in zip(attended, PLACES):
        row = pl.multiple_of(((y ^ dy) * 2 + (core ^ dc)) * width + (gx ^ dx) * cols, 16)
        pairs.append((ref, att_scr.at[pl.ds(row, cols)]))
    bounds = list(range(0, feats, 384))[:-1] + [feats]
    chunks = list(zip(bounds[:-1], bounds[1:]))
    for begin, end in chunks:
        for dc, parts in enumerate((weights[:3], weights[3:])):
            here = (y * 2 + (core ^ dc)) * width
            there = ((y ^ 1) * 2 + (core ^ dc)) * width
            rows = (here, there, there + parts[1].shape[0])
            for ref, row in zip(parts, rows):
                at = pl.ds(pl.multiple_of(row, 16), ref.shape[0])
                pairs.append((ref.at[:, begin:end], w_scr.at[at, begin:end]))
        if begin == 0:
            pairs.extend(token_copies(tokens, tok_scr))
    copies = run_copies(pairs, sem)
    column(gain[...], gain_scr)
    first = second = pivot = None
    waited = 0
    for i, (begin, end) in enumerate(chunks):
        needed = 8 + 6 + 8 + 6 * i
        for copy in copies[waited:needed]:
            copy.wait()
        waited = needed
        rows = dot_first(w_scr[:, begin:end], att_scr[...]) + side_by_side(tok_scr, slice(begin, end))
        rows = rows.astype(jnp.bfloat16)
        aft_scr[begin:end] = rows
        rows = rows.astype(jnp.float32)
        if pivot is None:
            pivot = rows[:1]
        rows = rows - pivot
        sums = fold(rows), fold(rows * rows)
        first, second = sums if first is None else (first + sums[0], second + sums[1])
    mean, scale = norm_of(pivot, first, second, feats)
    row = pl.multiple_of((y * 2 + core) * width, 16)
    mine = aft_scr[pl.ds(row, width)].astype(jnp.float32)
    half = total // 2
    own[...] = jnp.where(gx == 0, mine[:, :half], mine[:, half:]).astype(jnp.bfloat16)

    def write(i, carry):
        at = pl.ds(pl.multiple_of(i * STEP, STEP), STEP)
        rows = aft_scr[at, :].astype(jnp.float32) - mean
        normed[at, :] = (rows * scale * gain_scr[at, :1]).astype(jnp.bfloat16)
        return carry

    lax.fori_loop(0, feats // STEP, write, 0)


def up_kernel(normed, up_own, up_got, up_got_row, hidden, norm_scr, up_scr, sem):
    gx, y, core = position()
    plane = lax.axis_index("row") % 2
    feats, units = up_scr.shape
    depth = feats // 2
    chunk = units // 2
    own_rows = pl.ds(pl.multiple_of(gx * depth, 16), depth)
    other_rows = pl.ds(pl.multiple_of((1 - gx) * depth, 16), depth)
    pairs = [
        (normed, norm_scr),
        (up_own.at[:, pl.ds(pl.multiple_of(gx * units, 128), units)], up_scr.at[own_rows]),
        (up_got, up_scr.at[other_rows, pl.ds(pl.multiple_of(plane * chunk, 128), chunk)]),
        (up_got_row, up_scr.at[other_rows, pl.ds(pl.multiple_of((1 - plane) * chunk, 128), chunk)]),
    ]
    for copy in run_copies(pairs, sem):
        copy.wait()
    for begin in range(0, units, 256):
        rows = dot_first(up_scr[:, begin : begin + 256], norm_scr[...])
        rows = 0.5 * rows * (1.0 + lax.erf(rows * (0.5**0.5)))
        hidden[begin : begin + 256] = rows.astype(jnp.bfloat16)


def down_kernel(dc, hidden, down_own, *refs):
    got, outs, (hid_scr, down_scr, sem) = refs[:4], refs[-7:-3], refs[-3:]
    gx, y, core = position()
    plane = lax.axis_index("row") % 2
    depth = down_own.shape[0]
    units, total = hid_scr.shape
    chunk = units // 4
    own_rows = pl.ds(pl.multiple_of(gx * depth, 16), depth)
    other_rows = pl.ds(pl.multiple_of((1 - gx) * depth, 16), depth)
    pairs = [
        (hidden, hid_scr),
        (down_own.at[:, pl.ds(pl.multiple_of(gx * units, 128), units)], down_scr.at[own_rows]),
    ]
    for i, ref in enumerate(got):
        place = plane if i < 2 else 1 - plane
        at = pl.ds(pl.multiple_of((2 * place + i % 2) * chunk, 128), chunk)
        pairs.append((ref, down_scr.at[other_rows, at]))
    for copy in run_copies(pairs, sem):
        copy.wait()
    half = outs[0].shape[1]
    middle = total // 2
    for dy in range(2):
        for part in range(2):
            row = ((y ^ dy) * 2 + (core ^ dc)) * (2 * half) + part * half
            sums = matmul(down_scr[pl.ds(pl.multiple_of(row, 16), half)], hid_scr[...])
            left, right = sums[:, :middle], sums[:, middle:]
            for dx in range(2):
                group, other = (dx, dy) if part == 0 else (dy, dx)
                picked = jnp.where(gx == dx, left, right)
                outs[2 * (1 - group) + part][other] = picked.astype(jnp.bfloat16)


def last_sum_kernel(own, rest_x, rest_y, last_x, last_y, groups, out, picked):
    half, count = last_x.shape
    for i, (rest, source) in enumerate(((rest_x, last_x), (rest_y, last_y))):
        at = slice(i * half, (i + 1) * half)
        total = own[at].astype(jnp.float32) + rest[...].astype(jnp.float32) + source[...].astype(jnp.float32)
        out[at] = total.astype(jnp.bfloat16)
    for k in range(groups.shape[0]):
        place = lax.broadcasted_iota(jnp.int32, (count, groups.shape[1]), 0)
        chosen = jnp.where(place == groups[k : k + 1], 1.0, 0.0).astype(jnp.bfloat16)
        picked[k] = matmul(out[...], chosen).T.astype(jnp.bfloat16)


def merge_kernel(picked, weights, *refs):
    got, (keep, send, res_scr) = refs[:4], refs[-3:]
    gx, y, core = position()
    plane = lax.axis_index("row") % 2
    slots = weights.shape[0]
    width = keep.shape[1]
    own = matmul(picked[0], weights[0])
    for k in range(1, slots):
        own = own + matmul(picked[k], weights[k])
    other = None
    for i, ref in enumerate(got):
        place = plane if i < 2 else 1 - plane
        part = matmul(picked[2 * place + i % 2], ref[...])
        other = part if other is None else other + part
    res_scr[gx] = own.T
    res_scr[1 - gx] = other.T
    for dc, target in ((0, keep), (1, send)):
        row = pl.multiple_of((core ^ dc) * width, 16)
        for dy in range(2):
            target[dy] = res_scr[y ^ dy, pl.ds(row, width)].astype(jnp.bfloat16)


def add(*arrs):
    total = arrs[0].astype(jnp.float32)
    for arr in arrs[1:]:
        total = total + arr.astype(jnp.float32)
    return total.astype(jnp.bfloat16)


def return_kernel(*refs):
    tiles, sources, out = refs[:-2], refs[-2], refs[-1]
    row = lax.axis_index("row")
    count = sources.shape[1]
    total = None
    for step, tile in enumerate(tiles):
        slot = lax.broadcasted_iota(jnp.int32, (tile.shape[1], count), 0) + (row ^ step) * tile.shape[1]
        chosen = jnp.where(slot == sources[...], 1.0, 0.0).astype(jnp.bfloat16)
        part = matmul(tile[...], chosen)
        total = part if total is None else total + part
    out[...] = total.astype(jnp.bfloat16)


def call(kernel, operands, outs, far, scratch=(), flops=0, aliases=None, far_out=False, limit=VMEM_LIMIT):
    moved = sum(a.size * a.dtype.itemsize for a in operands)
    outs = tuple(jax.ShapeDtypeStruct(shape, dtype) for shape, dtype in outs)
    return pl.pallas_call(
        kernel,
        out_shape=outs,
        in_specs=[pl.BlockSpec(memory_space=pl.ANY if f else pltpu.VMEM) for f in far],
        out_specs=tuple(pl.BlockSpec(memory_space=pl.ANY if far_out else pltpu.VMEM) for _ in outs),
        scratch_shapes=list(scratch),
        input_output_aliases=aliases or {},
        compiler_params=pltpu.CompilerParams(vmem_limit_bytes=limit),
        cost_estimate=pl.CostEstimate(flops=flops, bytes_accessed=moved, transcendentals=0),
    )(*operands)


def after(held, passed):
    count = len(passed)
    return call(
        lambda *refs: None,
        (*passed, *held),
        [(a.shape, a.dtype) for a in passed],
        (True,) * (count + len(held)),
        aliases={i: i for i in range(count)},
        far_out=True,
    )


def rows_of(arr, begin, count):
    return lax.dynamic_slice_in_dim(arr, begin, count, 0)


def fast_body(
    tokens,
    segments,
    gain_attn,
    w_query,
    w_key,
    w_value,
    w_out,
    gain_mlp,
    w_up,
    w_down,
    w_merge,
    merge_groups,
    sources,
):
    gx = lax.axis_index("gx")
    plane = lax.axis_index("row") % 2
    tok = tokens[0].T
    width, count = tok.shape
    feats = 4 * width
    depth = feats // 2
    half = width // 2
    cols = w_query.shape[1] // 2
    total_cols = 3 * cols
    sixteen = jnp.bfloat16
    total = 2 * count
    gain_attn = gain_attn.reshape(1, -1)
    gain_mlp = gain_mlp.reshape(1, -1)
    down = w_down.T
    units = w_up.shape[1] // 2
    chunk = units // 2
    theirs = (1 - gx) * units + plane * chunk
    their_row = (1 - gx) * cols
    first = jnp.where(
        plane == 0, rows_of(w_query.T, their_row, cols), rows_of(w_value.T, their_row, cols)
    )

    over_x, over_y = swap_x(tok), swap_y(tok)
    qkv_got = swap_x(first)
    (key_piece,) = after((over_x,), (rows_of(w_key.T, their_row, cols),))
    qkv_got_key = swap_x(key_piece)
    held = [tok, over_y, over_x, swap_y(over_x)]
    tok_shards = held + [swap_core(part) for part in held]
    down_pieces = [
        lax.dynamic_slice_in_dim(down, theirs + i * (chunk // 2), chunk // 2, 1) for i in range(2)
    ]
    (up_piece,) = after((qkv_got,), (lax.dynamic_slice_in_dim(w_up, theirs, chunk, 1),))
    early = OUT_EARLY
    (out_early,) = after((over_y,), (w_out[:early],))
    (out_late,) = after((over_x, over_y, qkv_got), (w_out[early:],))
    out_over_y = [swap_y(out_early), swap_y(out_late)]
    qkv_got_row = swap_row(qkv_got, 1)
    up_piece, *down_pieces = after(
        (qkv_got_row, qkv_got_key, held[3], *tok_shards[4:7], out_over_y[0]), (up_piece, *down_pieces)
    )
    up_got = swap_x(up_piece)

    (attended,) = call(
        attention_kernel,
        (*tok_shards, gain_attn, w_query.T, w_key.T, w_value.T, qkv_got, qkv_got_row, qkv_got_key, segments),
        [((cols, total), sixteen)],
        (True,) * 8 + (False,) + (True,) * 6 + (False,),
        [
            pltpu.VMEM((2, feats, count), sixteen),
            pltpu.VMEM((feats, total), sixteen),
            pltpu.VMEM((2, total_cols, depth), sixteen),
            pltpu.VMEM((total_cols, total), jnp.float32),
            pltpu.VMEM((cols, total), jnp.float32),
            pltpu.VMEM((feats, 8), jnp.float32),
            pltpu.VMEM((total, 8), jnp.int32),
            pltpu.SemaphoreType.DMA((14,)),
        ],
        2 * total * feats * total_cols + 4 * total * total * cols,
    )
    attended, up_got = after((), (attended, up_got))
    over_x, over_y = swap_x(attended), swap_y(attended)
    up_got_row = swap_row(up_got, 1)
    slots = w_merge.shape[0]
    merge_pieces = [rows_of(w_merge, plane * (slots // 2) + i, 1)[0] for i in range(2)]
    *out_over_y, down_piece_a, down_piece_b, merge_a, merge_b = after(
        (over_x, over_y), (*out_over_y, *down_pieces, *merge_pieces)
    )
    merge_pieces = [merge_a, merge_b]
    down_got_a, down_got_b = swap_x(down_piece_a), swap_x(down_piece_b)
    (diagonal,) = after((down_got_a, up_got_row), (swap_y(over_x),))
    held = [attended, over_y, over_x, diagonal]
    att_shards = held + [swap_core(part) for part in held]
    out_parts = [w_out, *out_over_y]
    out_parts = out_parts + [swap_core(part) for part in out_parts]
    down_got_a_row = swap_row(down_got_a, 1)
    normed, own = call(
        project_kernel,
        (*tok_shards, *att_shards, *out_parts, gain_mlp, down_got_a, up_got_row),
        [((feats, total), sixteen), ((width, count), sixteen)],
        (True,) * 22 + (False, True, True),
        [
            pltpu.VMEM((2, feats, count), sixteen),
            pltpu.VMEM((feats, total), sixteen),
            pltpu.VMEM((feats, feats), sixteen),
            pltpu.VMEM((feats, total), sixteen),
            pltpu.VMEM((feats, 8), jnp.float32),
            pltpu.SemaphoreType.DMA((40,)),
        ],
        2 * total * feats * feats,
    )
    merge_got = [swap_x(part) for part in merge_pieces]
    normed, down_got_b = after((), (normed, down_got_b))
    (hidden,) = call(
        up_kernel,
        (normed, w_up, up_got, up_got_row),
        [((units, total), sixteen)],
        (True,) * 4,
        [
            pltpu.VMEM((feats, total), sixteen),
            pltpu.VMEM((feats, units), sixteen),
            pltpu.SemaphoreType.DMA((4,)),
        ],
        2 * total * feats * units,
        limit=SMALL_LIMIT,
    )
    down_got_b_row = swap_row(down_got_b, 1)
    hidden, merge_got[0] = after((), (hidden, merge_got[0]))
    pair = ((2, half, count), sixteen)

    def down_part(dc, *others):
        return call(
            functools.partial(down_kernel, dc),
            (hidden, down, down_got_a, down_got_b, down_got_a_row, down_got_b_row, *others),
            [pair] * 4,
            (True,) * (6 + len(others)),
            [
                pltpu.VMEM((units, total), sixteen),
                pltpu.VMEM((feats, units), sixteen),
                pltpu.SemaphoreType.DMA((6,)),
            ],
            total * feats * units,
            limit=SMALL_LIMIT,
        )

    send = down_part(1)
    got = [swap_core(part) for part in send]
    merge_got_row = [swap_row(part, 1) for part in merge_got]
    keep = down_part(0, *send)
    keep = after((merge_got[1], merge_got_row[0]), keep)
    from_x = swap_x(add(keep[0], got[0]))
    from_y = swap_y(add(keep[1], got[1]))
    rest_x, rest_y = add(keep[2], got[2], from_x), add(keep[3], got[3], from_y)
    last_x, last_y = swap_y(rest_x[1]), swap_x(rest_y[1])
    merged_count = merge_groups.shape[1]
    after_mlp, picked = call(
        last_sum_kernel,
        (own, rest_x[0], rest_y[0], last_x, last_y, merge_groups[0].T),
        [((width, count), sixteen), ((slots, merged_count, width), sixteen)],
        (False,) * 6,
        (),
        2 * count * width * count,
        limit=SMALL_LIMIT,
    )
    keep, send = call(
        merge_kernel,
        (picked, w_merge, *merge_got, *merge_got_row),
        [((2, width, merged_count), sixteen)] * 2,
        (False,) * 6,
        [pltpu.VMEM((2, depth, merged_count), jnp.float32)],
        2 * count * width * feats,
        limit=SMALL_LIMIT,
    )
    mine = add(keep, swap_core(send))
    merged = add(mine[0], swap_y(mine[1]))
    tiles = [merged] + [swap_row(merged, step) for step in range(1, lax.axis_size("row"))]
    (returned,) = call(
        return_kernel,
        (*tiles, sources),
        [((width, merged_count), sixteen)],
        (False,) * (len(tiles) + 1),
        (),
        2 * count * width * merged_count,
        limit=SMALL_LIMIT,
    )
    return (after_mlp.T[None], returned.T[None])


def solution(mesh):
    placed = (
        P("row", "gx", "gy"),
        P("row", None),
        P(),
        P("gx", "gy"),
        P("gx", "gy"),
        P("gx", "gy"),
        P("gy", None),
        P(),
        P("gx", "gy"),
        P("gy", "gx"),
        P(None, "gy", "gx"),
        P("row", "gx", None),
        P("row", "gx"),
    )
    small = mesh.shape["gx"] == 2 and mesh.shape["gy"] == 4 and mesh.shape["row"] in (2, 4)
    return jax.shard_map(
        fast_body if small else general_body,
        mesh=mesh,
        in_specs=placed,
        out_specs=(P("row", "gx", "gy"), P("row", "gx", "gy")),
        check_vma=False,
    )
```

```python
import functools

import jax
import jax.numpy as jnp
from jax import lax
from jax.experimental import pallas as pl
from jax.experimental.pallas import tpu as pltpu
from jax.sharding import PartitionSpec as P

HD = 104


EPS = 1e-06
NEG = -1e30
VMEM_LIMIT = 30 * 1024 * 1024
SMALL_LIMIT = 24 * 1024 * 1024
LOG2_E = 1.4426950408889634


def normalize(tok_rows, gain):
    tok_rows = tok_rows.astype(jnp.float32)
    row_mean = jnp.mean(tok_rows, axis=-1, keepdims=True)
    centred = tok_rows - row_mean
    row_var = jnp.mean(centred * centred, axis=-1, keepdims=True)
    return (centred * lax.rsqrt(row_var + EPS) * gain).astype(jnp.bfloat16)


def general_body(
    tokens,
    segments,
    gain_attn,
    w_query,
    w_key,
    w_value,
    w_out,
    gain_mlp,
    w_up,
    w_down,
    w_merge,
    merge_groups,
    sources,
):
    tok_local = tokens[0]
    row_count = tok_local.shape[0]
    seg_all = segments[0]
    col_count = w_query.shape[1]
    head_count = col_count // HD
    scale = HD ** (-0.5)
    gathered = lax.all_gather(tok_local, "gy", axis=1, tiled=True)
    normed = normalize(gathered, gain_attn)
    pieces = (
        lax.all_gather(w_query, "gx", axis=0, tiled=True),
        lax.all_gather(w_key, "gx", axis=0, tiled=True),
        lax.all_gather(w_value, "gx", axis=0, tiled=True),
    )
    feat_part = normed
    q_sum = jnp.dot(feat_part, pieces[0], preferred_element_type=jnp.float32)
    k_sum = jnp.dot(feat_part, pieces[1], preferred_element_type=jnp.float32)
    v_sum = jnp.dot(feat_part, pieces[2], preferred_element_type=jnp.float32)
    queries = q_sum.astype(jnp.bfloat16).reshape(row_count, head_count, HD)
    key_rows = k_sum.astype(jnp.bfloat16)
    value_rows = v_sum.astype(jnp.bfloat16)
    own_seg = lax.dynamic_slice_in_dim(seg_all, lax.axis_index("gx") * row_count, row_count)
    start_state = (
        jnp.full((row_count, head_count), NEG, jnp.float32),
        jnp.zeros((row_count, head_count), jnp.float32),
        jnp.zeros((row_count, head_count, HD), jnp.float32),
    )
    pieces = (
        lax.all_gather(key_rows, "gx", axis=0, tiled=True),
        lax.all_gather(value_rows, "gx", axis=0, tiled=True),
    )
    key_count = pieces[0].shape[0]
    block_len = min(row_count, key_count)
    block_total = key_count // block_len

    def one_block(step, old):
        block_keys = lax.dynamic_slice_in_dim(pieces[0], step * block_len, block_len, 0)
        block_values = lax.dynamic_slice_in_dim(pieces[1], step * block_len, block_len, 0)
        key_seg = lax.dynamic_slice_in_dim(seg_all, step * block_len, block_len)
        row_top, row_total, weighted = old
        key_heads = block_keys.reshape(block_len, head_count, HD)
        value_heads = block_values.reshape(block_len, head_count, HD)
        scores = (
            jnp.einsum("qhd,khd->qhk", queries, key_heads, preferred_element_type=jnp.float32)
            * scale
        )
        same_seg = (own_seg[:, None] == key_seg[None, :])[:, None, :]
        scores = jnp.where(same_seg, scores, NEG)
        new_top = jnp.maximum(row_top, jnp.max(scores, axis=-1))
        weights = jnp.where(same_seg, jnp.exp(scores - new_top[:, :, None]), 0.0)
        rescale = jnp.exp(row_top - new_top)
        row_total = row_total * rescale + jnp.sum(weights, axis=-1)
        weighted = weighted * rescale[:, :, None] + jnp.einsum(
            "qhk,khd->qhd",
            weights.astype(jnp.bfloat16),
            value_heads,
            preferred_element_type=jnp.float32,
        )
        return (new_top, row_total, weighted)

    row_top, row_total, weighted = lax.fori_loop(0, block_total, one_block, start_state)
    attended = (weighted / row_total[:, :, None]).reshape(row_count, col_count).astype(jnp.bfloat16)
    out_cols = lax.all_to_all(w_out, "gy", split_axis=1, concat_axis=0, tiled=True)
    attn_out = jnp.dot(
        lax.all_gather(attended, "gy", axis=1, tiled=True),
        out_cols,
        preferred_element_type=jnp.float32,
    )
    after_attn = (tok_local.astype(jnp.float32) + attn_out).astype(jnp.bfloat16)
    gathered_mlp = lax.all_gather(after_attn, "gy", axis=1, tiled=True)
    normed_mlp = normalize(gathered_mlp, gain_mlp)
    feat_part = normed_mlp
    hidden_sum = jnp.dot(
        feat_part,
        lax.all_gather(w_up, "gx", axis=0, tiled=True),
        preferred_element_type=jnp.float32,
    )
    hidden = jax.nn.gelu(hidden_sum, approximate=False).astype(jnp.bfloat16)
    partials = jnp.dot(
        hidden, lax.all_gather(w_down, "gx", axis=1, tiled=True), preferred_element_type=jnp.float32
    )
    mlp_out = lax.psum_scatter(
        partials.astype(jnp.bfloat16), "gy", scatter_dimension=1, tiled=True
    ).astype(jnp.float32)
    after_mlp = (after_attn.astype(jnp.float32) + mlp_out).astype(jnp.bfloat16)
    picked = after_mlp[merge_groups[0]]
    merge_terms = jnp.einsum(
        "mkc,kcn->mn",
        picked,
        lax.all_gather(w_merge, "gx", axis=2, tiled=True),
        preferred_element_type=jnp.float32,
    )
    merged = lax.psum_scatter(
        merge_terms.astype(jnp.bfloat16), "gy", scatter_dimension=1, tiled=True
    )
    pooled = lax.all_gather(merged[None], "row", axis=0, tiled=True)
    stacked = pooled.reshape(-1, merged.shape[1])
    returned = stacked[sources[0]]
    return (after_mlp[None], returned[None])


def swap_x(arr):
    return lax.ppermute(arr, "gx", [(0, 1), (1, 0)])


def swap_y(arr):
    return lax.ppermute(arr, "gy", [(i, i ^ 2) for i in range(4)])


def swap_core(arr):
    return lax.ppermute(arr, "gy", [(i, i ^ 1) for i in range(4)])


def swap_row(arr, step):
    count = lax.axis_size("row")
    return lax.ppermute(arr, "row", [(i, i ^ step) for i in range(count)])


def gather_eight(own):
    over_x = swap_x(own)
    over_y = swap_y(own)
    held = [own, over_y, over_x, swap_y(over_x)]
    return held + [swap_core(part) for part in held]


PLACES = tuple((dx, dy, dc) for dc in (0, 1) for dx in (0, 1) for dy in (0, 1))


def position():
    gx = lax.axis_index("gx")
    gy = lax.axis_index("gy")
    return gx, gy // 2, gy % 2


def run_copies(pairs, sem):
    copies = [pltpu.make_async_copy(src, dst, sem.at[i]) for i, (src, dst) in enumerate(pairs)]
    for copy in copies:
        copy.start()
    return copies


def token_copies(refs, tok_scr):
    gx, y, core = position()
    width = refs[0].shape[0]
    pairs = []
    for ref, (dx, dy, dc) in zip(refs, PLACES):
        row = pl.multiple_of(((y ^ dy) * 2 + (core ^ dc)) * width, 16)
        pairs.append((ref, tok_scr.at[gx ^ dx, pl.ds(row, width)]))
    return pairs


STEP = 64


def column(row, scratch):
    scratch[...] = jnp.broadcast_to(row, (8, row.shape[1])).T


def side_by_side(pair, at):
    return jnp.concatenate([pair[0, at].astype(jnp.float32), pair[1, at].astype(jnp.float32)], axis=1)


def fold(rows):
    return jnp.sum(rows.reshape(rows.shape[0] // 8, 8, rows.shape[1]), axis=0)


def norm_of(pivot, first, second, feats):
    shift = jnp.sum(first, axis=0, keepdims=True) / feats
    variance = jnp.maximum(jnp.sum(second, axis=0, keepdims=True) / feats - shift * shift, 0.0)
    return pivot + shift, lax.rsqrt(variance + EPS)


def norm_tokens(pair, gain, out):
    _, feats, count = pair.shape
    steps = feats // STEP
    pivots = [pair[g, :16].astype(jnp.float32)[:1] for g in range(2)]

    def add_up(i, totals):
        at = pl.ds(pl.multiple_of(i * STEP, STEP), STEP)
        new = []
        for g in range(2):
            rows = pair[g, at].astype(jnp.float32) - pivots[g]
            new.append(totals[2 * g] + fold(rows))
            new.append(totals[2 * g + 1] + fold(rows * rows))
        return tuple(new)

    zero = jnp.zeros((8, count), jnp.float32)
    totals = lax.fori_loop(0, steps, add_up, (zero,) * 4)
    moments = [norm_of(pivots[g], totals[2 * g], totals[2 * g + 1], feats) for g in range(2)]
    mean, scale = (jnp.concatenate([moments[0][i], moments[1][i]], axis=1) for i in range(2))

    def write(i, carry):
        at = pl.ds(pl.multiple_of(i * STEP, STEP), STEP)
        rows = side_by_side(pair, at) - mean
        out[at, :] = (rows * scale * gain[at, :1]).astype(jnp.bfloat16)
        return carry

    lax.fori_loop(0, steps, write, 0)


def matmul(lhs, rhs):
    return jnp.dot(lhs, rhs, preferred_element_type=jnp.float32)


def dot_first(lhs, rhs):
    return lax.dot_general(lhs, rhs, (((0,), (0,)), ((), ())), preferred_element_type=jnp.float32)


def attention_kernel(*refs):
    shards = refs[:8]
    gain, w_query, w_key, w_value, w_got, w_got_row, w_got_key, segments = refs[8:16]
    out, tok_scr, norm_scr, w_scr, qkv_scr, att_scr, gain_scr, seg_scr, sem = refs[-9:]
    gx, y, core = position()
    plane = lax.axis_index("row") % 2
    cols = out.shape[0]
    pairs = token_copies(shards, tok_scr)
    own = pl.ds(pl.multiple_of(gx * cols, 16), cols)
    for i, ref in enumerate((w_query, w_key, w_value)):
        pairs.append((ref.at[own], w_scr.at[gx, pl.ds(i * cols, cols)]))
    pairs.append((w_got, w_scr.at[1 - gx, pl.ds(pl.multiple_of(2 * cols * plane, 16), cols)]))
    pairs.append((w_got_row, w_scr.at[1 - gx, pl.ds(pl.multiple_of(2 * cols * (1 - plane), 16), cols)]))
    pairs.append((w_got_key, w_scr.at[1 - gx, pl.ds(cols, cols)]))
    copies = run_copies(pairs, sem)
    column(gain[...], gain_scr)
    column(segments[...], seg_scr)
    for copy in copies[:8]:
        copy.wait()
    norm_tokens(tok_scr, gain_scr, norm_scr)
    for copy in copies[8:]:
        copy.wait()
    feats, total = norm_scr.shape
    depth = feats // 2
    qkv_scr[...] = matmul(w_scr[0], norm_scr[:depth]) + matmul(w_scr[1], norm_scr[depth:])
    scale = HD ** (-0.5) * LOG2_E
    for head in range(cols // HD):
        begin = head * HD
        keys = qkv_scr[cols + begin : cols + begin + HD].T.astype(jnp.bfloat16)
        values = qkv_scr[2 * cols + begin : 2 * cols + begin + HD].astype(jnp.bfloat16)
        for start in range(0, total, 256):
            at = slice(start, min(start + 256, total))
            scores = matmul(keys, (qkv_scr[begin : begin + HD, at] * scale).astype(jnp.bfloat16))
            scores = jnp.where(seg_scr[:, :1] == segments[:, at], scores, NEG)
            weights = jnp.exp2(scores - jnp.max(scores, axis=0, keepdims=True))
            row_total = jnp.sum(weights, axis=0, keepdims=True)
            att_scr[begin : begin + HD, at] = matmul(values, weights.astype(jnp.bfloat16)) / row_total
    out[...] = att_scr[...].astype(jnp.bfloat16)


def project_kernel(*refs):
    tokens, attended, weights, gain = refs[:8], refs[8:16], refs[16:20], refs[20]
    normed, own, tok_scr, att_scr, w_scr, aft_scr, gain_scr, sem = refs[-8:]
    gx, y, core = position()
    width = own.shape[0]
    cols = attended[0].shape[0]
    feats, total = att_scr.shape
    pairs = []
    for ref, (dx, dy, dc) in zip(attended, PLACES):
        row = pl.multiple_of(((y ^ dy) * 2 + (core ^ dc)) * width + (gx ^ dx) * cols, 16)
        pairs.append((ref, att_scr.at[pl.ds(row, cols)]))
    bounds = list(range(0, feats, 384))[:-1] + [feats]
    chunks = list(zip(bounds[:-1], bounds[1:]))
    for begin, end in chunks:
        for dc, parts in enumerate((weights[:2], weights[2:])):
            here = (y * 2 + (core ^ dc)) * width
            there = ((y ^ 1) * 2 + (core ^ dc)) * width
            for ref, row in zip(parts, (here, there)):
                at = pl.ds(pl.multiple_of(row, 16), ref.shape[0])
                pairs.append((ref.at[:, begin:end], w_scr.at[at, begin:end]))
        if begin == 0:
            pairs.extend(token_copies(tokens, tok_scr))
    copies = run_copies(pairs, sem)
    column(gain[...], gain_scr)
    first = second = pivot = None
    waited = 0
    for i, (begin, end) in enumerate(chunks):
        needed = 8 + 4 + 8 + 4 * i
        for copy in copies[waited:needed]:
            copy.wait()
        waited = needed
        rows = dot_first(w_scr[:, begin:end], att_scr[...]) + side_by_side(tok_scr, slice(begin, end))
        rows = rows.astype(jnp.bfloat16)
        aft_scr[begin:end] = rows
        rows = rows.astype(jnp.float32)
        if pivot is None:
            pivot = rows[:1]
        rows = rows - pivot
        sums = fold(rows), fold(rows * rows)
        first, second = sums if first is None else (first + sums[0], second + sums[1])
    mean, scale = norm_of(pivot, first, second, feats)
    row = pl.multiple_of((y * 2 + core) * width, 16)
    mine = aft_scr[pl.ds(row, width)].astype(jnp.float32)
    half = total // 2
    own[...] = jnp.where(gx == 0, mine[:, :half], mine[:, half:]).astype(jnp.bfloat16)

    def write(i, carry):
        at = pl.ds(pl.multiple_of(i * STEP, STEP), STEP)
        rows = aft_scr[at, :].astype(jnp.float32) - mean
        normed[at, :] = (rows * scale * gain_scr[at, :1]).astype(jnp.bfloat16)
        return carry

    lax.fori_loop(0, feats // STEP, write, 0)


def chunk_places(got, piece):
    plane = lax.axis_index("row") % 2
    for i, ref in enumerate(got):
        place = plane if i < 2 else 1 - plane
        yield ref, pl.ds(pl.multiple_of((2 * place + i % 2) * piece, 128), piece)


def up_kernel(normed, up_own, *refs):
    got, (hidden, norm_scr, up_scr, sem) = refs[:4], refs[4:]
    gx, y, core = position()
    feats, units = up_scr.shape
    depth = feats // 2
    own_rows = pl.ds(pl.multiple_of(gx * depth, 16), depth)
    other_rows = pl.ds(pl.multiple_of((1 - gx) * depth, 16), depth)
    pairs = [
        (normed, norm_scr),
        (up_own.at[:, pl.ds(pl.multiple_of(gx * units, 128), units)], up_scr.at[own_rows]),
    ]
    for ref, at in chunk_places(got, units // 4):
        pairs.append((ref, up_scr.at[other_rows, at]))
    for copy in run_copies(pairs, sem):
        copy.wait()
    for begin in range(0, units, 256):
        rows = dot_first(up_scr[:, begin : begin + 256], norm_scr[...])
        rows = 0.5 * rows * (1.0 + lax.erf(rows * (0.5**0.5)))
        hidden[begin : begin + 256] = rows.astype(jnp.bfloat16)


def down_kernel(dc, hidden, down_own, *refs):
    got, outs, (hid_scr, down_scr, sem) = refs[:4], refs[-7:-3], refs[-3:]
    gx, y, core = position()
    depth = down_own.shape[0]
    units, total = hid_scr.shape
    own_rows = pl.ds(pl.multiple_of(gx * depth, 16), depth)
    other_rows = pl.ds(pl.multiple_of((1 - gx) * depth, 16), depth)
    pairs = [
        (hidden, hid_scr),
        (down_own.at[:, pl.ds(pl.multiple_of(gx * units, 128), units)], down_scr.at[own_rows]),
    ]
    for ref, at in chunk_places(got, units // 4):
        pairs.append((ref, down_scr.at[other_rows, at]))
    for copy in run_copies(pairs, sem):
        copy.wait()
    half = outs[0].shape[1]
    middle = total // 2
    for dy in range(2):
        for part in range(2):
            row = ((y ^ dy) * 2 + (core ^ dc)) * (2 * half) + part * half
            sums = matmul(down_scr[pl.ds(pl.multiple_of(row, 16), half)], hid_scr[...])
            left, right = sums[:, :middle], sums[:, middle:]
            for dx in range(2):
                group, other = (dx, dy) if part == 0 else (dy, dx)
                picked = jnp.where(gx == dx, left, right)
                outs[2 * (1 - group) + part][other] = picked.astype(jnp.bfloat16)


def last_sum_kernel(own, rest_x, rest_y, last_x, last_y, groups, out, picked):
    half, count = last_x.shape
    for i, (rest, source) in enumerate(((rest_x, last_x), (rest_y, last_y))):
        at = slice(i * half, (i + 1) * half)
        total = own[at].astype(jnp.float32) + rest[...].astype(jnp.float32) + source[...].astype(jnp.float32)
        out[at] = total.astype(jnp.bfloat16)
    for k in range(groups.shape[0]):
        place = lax.broadcasted_iota(jnp.int32, (count, groups.shape[1]), 0)
        chosen = jnp.where(place == groups[k : k + 1], 1.0, 0.0).astype(jnp.bfloat16)
        picked[k] = matmul(out[...], chosen).T.astype(jnp.bfloat16)


def merge_kernel(picked, weights, *refs):
    got, (keep, send, res_scr) = refs[:4], refs[-3:]
    gx, y, core = position()
    plane = lax.axis_index("row") % 2
    slots = weights.shape[0]
    width = keep.shape[1]
    own = matmul(picked[0], weights[0])
    for k in range(1, slots):
        own = own + matmul(picked[k], weights[k])
    other = None
    for i, ref in enumerate(got):
        place = plane if i < 2 else 1 - plane
        part = matmul(picked[2 * place + i % 2], ref[...])
        other = part if other is None else other + part
    res_scr[gx] = own.T
    res_scr[1 - gx] = other.T
    for dc, target in ((0, keep), (1, send)):
        row = pl.multiple_of((core ^ dc) * width, 16)
        for dy in range(2):
            target[dy] = res_scr[y ^ dy, pl.ds(row, width)].astype(jnp.bfloat16)


def add(*arrs):
    total = arrs[0].astype(jnp.float32)
    for arr in arrs[1:]:
        total = total + arr.astype(jnp.float32)
    return total.astype(jnp.bfloat16)


def return_kernel(*refs):
    tiles, sources, out = refs[:-2], refs[-2], refs[-1]
    row = lax.axis_index("row")
    count = sources.shape[1]
    total = None
    for step, tile in enumerate(tiles):
        slot = lax.broadcasted_iota(jnp.int32, (tile.shape[1], count), 0) + (row ^ step) * tile.shape[1]
        chosen = jnp.where(slot == sources[...], 1.0, 0.0).astype(jnp.bfloat16)
        part = matmul(tile[...], chosen)
        total = part if total is None else total + part
    out[...] = total.astype(jnp.bfloat16)


def call(kernel, operands, outs, far, scratch=(), flops=0, aliases=None, far_out=False, limit=VMEM_LIMIT):
    moved = sum(a.size * a.dtype.itemsize for a in operands)
    outs = tuple(jax.ShapeDtypeStruct(shape, dtype) for shape, dtype in outs)
    return pl.pallas_call(
        kernel,
        out_shape=outs,
        in_specs=[pl.BlockSpec(memory_space=pl.ANY if f else pltpu.VMEM) for f in far],
        out_specs=tuple(pl.BlockSpec(memory_space=pl.ANY if far_out else pltpu.VMEM) for _ in outs),
        scratch_shapes=list(scratch),
        input_output_aliases=aliases or {},
        compiler_params=pltpu.CompilerParams(vmem_limit_bytes=limit),
        cost_estimate=pl.CostEstimate(flops=flops, bytes_accessed=moved, transcendentals=0),
    )(*operands)


def after(held, passed):
    count = len(passed)
    return call(
        lambda *refs: None,
        (*passed, *held),
        [(a.shape, a.dtype) for a in passed],
        (True,) * (count + len(held)),
        aliases={i: i for i in range(count)},
        far_out=True,
    )


def rows_of(arr, begin, count):
    return lax.dynamic_slice_in_dim(arr, begin, count, 0)


def fast_body(
    tokens,
    segments,
    gain_attn,
    w_query,
    w_key,
    w_value,
    w_out,
    gain_mlp,
    w_up,
    w_down,
    w_merge,
    merge_groups,
    sources,
):
    gx = lax.axis_index("gx")
    plane = lax.axis_index("row") % 2
    tok = tokens[0].T
    width, count = tok.shape
    feats = 4 * width
    depth = feats // 2
    half = width // 2
    cols = w_query.shape[1] // 2
    total_cols = 3 * cols
    sixteen = jnp.bfloat16
    total = 2 * count
    gain_attn = gain_attn.reshape(1, -1)
    gain_mlp = gain_mlp.reshape(1, -1)
    down = w_down.T
    units = w_up.shape[1] // 2
    chunk = units // 2
    theirs = (1 - gx) * units + plane * chunk
    their_row = (1 - gx) * cols
    first = jnp.where(
        plane == 0, rows_of(w_query.T, their_row, cols), rows_of(w_value.T, their_row, cols)
    )

    over_x, over_y = swap_x(tok), swap_y(tok)
    qkv_got = swap_x(first)
    (key_piece,) = after((qkv_got,), (rows_of(w_key.T, their_row, cols),))
    qkv_got_key = swap_x(key_piece)
    held = [tok, over_y, over_x, swap_y(over_x)]
    tok_shards = held + [swap_core(part) for part in held]
    piece = chunk // 2
    down_a, down_b = (lax.dynamic_slice_in_dim(down, theirs + i * piece, piece, 1) for i in range(2))
    up_a, up_b = (lax.dynamic_slice_in_dim(w_up, theirs + i * piece, piece, 1) for i in range(2))
    (up_a,) = after((qkv_got, over_x), (up_a,))
    up_got_a = swap_x(up_a)
    qkv_got_row = swap_row(qkv_got, 1)
    (out_piece,) = after((held[3],), (w_out,))
    out_over_y = [swap_y(out_piece)]
    up_b, down_a, down_b = after(
        (qkv_got_row, qkv_got_key, held[3], *tok_shards[4:7], out_piece), (up_b, down_a, down_b)
    )
    up_got_b, down_got_a = swap_x(up_b), swap_x(down_a)
    up_got_a_row = swap_row(up_got_a, 1)

    (attended,) = call(
        attention_kernel,
        (*tok_shards, gain_attn, w_query.T, w_key.T, w_value.T, qkv_got, qkv_got_row, qkv_got_key, segments, up_got_a),
        [((cols, total), sixteen)],
        (True,) * 8 + (False,) + (True,) * 6 + (False, True),
        [
            pltpu.VMEM((2, feats, count), sixteen),
            pltpu.VMEM((feats, total), sixteen),
            pltpu.VMEM((2, total_cols, depth), sixteen),
            pltpu.VMEM((total_cols, total), jnp.float32),
            pltpu.VMEM((cols, total), jnp.float32),
            pltpu.VMEM((feats, 8), jnp.float32),
            pltpu.VMEM((total, 8), jnp.int32),
            pltpu.SemaphoreType.DMA((14,)),
        ],
        2 * total * feats * total_cols + 4 * total * total * cols,
    )
    attended, up_got_b, down_got_a = after((up_got_a_row,), (attended, up_got_b, down_got_a))
    over_x, over_y = swap_x(attended), swap_y(attended)
    up_got_b_row, down_got_a_row = swap_row(up_got_b, 1), swap_row(down_got_a, 1)
    slots = w_merge.shape[0]
    merge_pieces = [rows_of(w_merge, plane * (slots // 2) + i, 1)[0] for i in range(2)]
    *out_over_y, down_b = after((over_x, over_y, up_got_b_row), (*out_over_y, down_b))
    down_got_b = swap_x(down_b)
    diagonal, *merge_pieces = after((down_got_a_row, down_got_b), (swap_y(over_x), *merge_pieces))
    held = [attended, over_y, over_x, diagonal]
    att_shards = held + [swap_core(part) for part in held]
    out_parts = [w_out, *out_over_y]
    out_parts = out_parts + [swap_core(part) for part in out_parts]
    down_got_b_row = swap_row(down_got_b, 1)
    normed, own = call(
        project_kernel,
        (*tok_shards, *att_shards, *out_parts, gain_mlp, down_got_b, down_got_a_row),
        [((feats, total), sixteen), ((width, count), sixteen)],
        (True,) * 20 + (False, True, True),
        [
            pltpu.VMEM((2, feats, count), sixteen),
            pltpu.VMEM((feats, total), sixteen),
            pltpu.VMEM((feats, feats), sixteen),
            pltpu.VMEM((feats, total), sixteen),
            pltpu.VMEM((feats, 8), jnp.float32),
            pltpu.SemaphoreType.DMA((32,)),
        ],
        2 * total * feats * feats,
    )
    merge_got = [swap_x(part) for part in merge_pieces]
    normed, merge_got[0] = after((), (normed, merge_got[0]))
    (hidden,) = call(
        up_kernel,
        (normed, w_up, up_got_a, up_got_b, up_got_a_row, up_got_b_row),
        [((units, total), sixteen)],
        (True,) * 6,
        [
            pltpu.VMEM((feats, total), sixteen),
            pltpu.VMEM((feats, units), sixteen),
            pltpu.SemaphoreType.DMA((6,)),
        ],
        2 * total * feats * units,
        limit=SMALL_LIMIT,
    )
    pair = ((2, half, count), sixteen)

    def down_part(dc, *others):
        return call(
            functools.partial(down_kernel, dc),
            (hidden, down, down_got_a, down_got_b, down_got_a_row, down_got_b_row, *others),
            [pair] * 4,
            (True,) * (6 + len(others)),
            [
                pltpu.VMEM((units, total), sixteen),
                pltpu.VMEM((feats, units), sixteen),
                pltpu.SemaphoreType.DMA((6,)),
            ],
            total * feats * units,
            limit=SMALL_LIMIT,
        )

    send = down_part(1)
    got = [swap_core(part) for part in send]
    merge_got_row = [swap_row(part, 1) for part in merge_got]
    keep = down_part(0, *send)
    keep = after((merge_got[1], merge_got_row[0]), keep)
    from_x = swap_x(add(keep[0], got[0]))
    from_y = swap_y(add(keep[1], got[1]))
    rest_x, rest_y = add(keep[2], got[2], from_x), add(keep[3], got[3], from_y)
    last_x, last_y = swap_y(rest_x[1]), swap_x(rest_y[1])
    merged_count = merge_groups.shape[1]
    after_mlp, picked = call(
        last_sum_kernel,
        (own, rest_x[0], rest_y[0], last_x, last_y, merge_groups[0].T),
        [((width, count), sixteen), ((slots, merged_count, width), sixteen)],
        (False,) * 6,
        (),
        2 * count * width * count,
        limit=SMALL_LIMIT,
    )
    keep, send = call(
        merge_kernel,
        (picked, w_merge, *merge_got, *merge_got_row),
        [((2, width, merged_count), sixteen)] * 2,
        (False,) * 6,
        [pltpu.VMEM((2, depth, merged_count), jnp.float32)],
        2 * count * width * feats,
        limit=SMALL_LIMIT,
    )
    mine = add(keep, swap_core(send))
    merged = add(mine[0], swap_y(mine[1]))
    tiles = [merged] + [swap_row(merged, step) for step in range(1, lax.axis_size("row"))]
    (returned,) = call(
        return_kernel,
        (*tiles, sources),
        [((width, merged_count), sixteen)],
        (False,) * (len(tiles) + 1),
        (),
        2 * count * width * merged_count,
        limit=SMALL_LIMIT,
    )
    return (after_mlp.T[None], returned.T[None])


def solution(mesh):
    placed = (
        P("row", "gx", "gy"),
        P("row", None),
        P(),
        P("gx", "gy"),
        P("gx", "gy"),
        P("gx", "gy"),
        P("gy", None),
        P(),
        P("gx", "gy"),
        P("gy", "gx"),
        P(None, "gy", "gx"),
        P("row", "gx", None),
        P("row", "gx"),
    )
    small = mesh.shape["gx"] == 2 and mesh.shape["gy"] == 4 and mesh.shape["row"] in (2, 4)
    return jax.shard_map(
        fast_body if small else general_body,
        mesh=mesh,
        in_specs=placed,
        out_specs=(P("row", "gx", "gy"), P("row", "gx", "gy")),
        check_vma=False,
    )
```

```python
import functools

import jax
import jax.numpy as jnp
from jax import lax
from jax.experimental import pallas as pl
from jax.experimental.pallas import tpu as pltpu
from jax.sharding import PartitionSpec as P

HD = 104


EPS = 1e-06
NEG = -1e30
VMEM_LIMIT = 30 * 1024 * 1024
SMALL_LIMIT = 24 * 1024 * 1024
LOG2_E = 1.4426950408889634


def normalize(tok_rows, gain):
    tok_rows = tok_rows.astype(jnp.float32)
    row_mean = jnp.mean(tok_rows, axis=-1, keepdims=True)
    centred = tok_rows - row_mean
    row_var = jnp.mean(centred * centred, axis=-1, keepdims=True)
    return (centred * lax.rsqrt(row_var + EPS) * gain).astype(jnp.bfloat16)


def general_body(
    tokens,
    segments,
    gain_attn,
    w_query,
    w_key,
    w_value,
    w_out,
    gain_mlp,
    w_up,
    w_down,
    w_merge,
    merge_groups,
    sources,
):
    tok_local = tokens[0]
    row_count = tok_local.shape[0]
    seg_all = segments[0]
    col_count = w_query.shape[1]
    head_count = col_count // HD
    scale = HD ** (-0.5)
    gathered = lax.all_gather(tok_local, "gy", axis=1, tiled=True)
    normed = normalize(gathered, gain_attn)
    pieces = (
        lax.all_gather(w_query, "gx", axis=0, tiled=True),
        lax.all_gather(w_key, "gx", axis=0, tiled=True),
        lax.all_gather(w_value, "gx", axis=0, tiled=True),
    )
    feat_part = normed
    q_sum = jnp.dot(feat_part, pieces[0], preferred_element_type=jnp.float32)
    k_sum = jnp.dot(feat_part, pieces[1], preferred_element_type=jnp.float32)
    v_sum = jnp.dot(feat_part, pieces[2], preferred_element_type=jnp.float32)
    queries = q_sum.astype(jnp.bfloat16).reshape(row_count, head_count, HD)
    key_rows = k_sum.astype(jnp.bfloat16)
    value_rows = v_sum.astype(jnp.bfloat16)
    own_seg = lax.dynamic_slice_in_dim(seg_all, lax.axis_index("gx") * row_count, row_count)
    start_state = (
        jnp.full((row_count, head_count), NEG, jnp.float32),
        jnp.zeros((row_count, head_count), jnp.float32),
        jnp.zeros((row_count, head_count, HD), jnp.float32),
    )
    pieces = (
        lax.all_gather(key_rows, "gx", axis=0, tiled=True),
        lax.all_gather(value_rows, "gx", axis=0, tiled=True),
    )
    key_count = pieces[0].shape[0]
    block_len = min(row_count, key_count)
    block_total = key_count // block_len

    def one_block(step, old):
        block_keys = lax.dynamic_slice_in_dim(pieces[0], step * block_len, block_len, 0)
        block_values = lax.dynamic_slice_in_dim(pieces[1], step * block_len, block_len, 0)
        key_seg = lax.dynamic_slice_in_dim(seg_all, step * block_len, block_len)
        row_top, row_total, weighted = old
        key_heads = block_keys.reshape(block_len, head_count, HD)
        value_heads = block_values.reshape(block_len, head_count, HD)
        scores = (
            jnp.einsum("qhd,khd->qhk", queries, key_heads, preferred_element_type=jnp.float32)
            * scale
        )
        same_seg = (own_seg[:, None] == key_seg[None, :])[:, None, :]
        scores = jnp.where(same_seg, scores, NEG)
        new_top = jnp.maximum(row_top, jnp.max(scores, axis=-1))
        weights = jnp.where(same_seg, jnp.exp(scores - new_top[:, :, None]), 0.0)
        rescale = jnp.exp(row_top - new_top)
        row_total = row_total * rescale + jnp.sum(weights, axis=-1)
        weighted = weighted * rescale[:, :, None] + jnp.einsum(
            "qhk,khd->qhd",
            weights.astype(jnp.bfloat16),
            value_heads,
            preferred_element_type=jnp.float32,
        )
        return (new_top, row_total, weighted)

    row_top, row_total, weighted = lax.fori_loop(0, block_total, one_block, start_state)
    attended = (weighted / row_total[:, :, None]).reshape(row_count, col_count).astype(jnp.bfloat16)
    out_cols = lax.all_to_all(w_out, "gy", split_axis=1, concat_axis=0, tiled=True)
    attn_out = jnp.dot(
        lax.all_gather(attended, "gy", axis=1, tiled=True),
        out_cols,
        preferred_element_type=jnp.float32,
    )
    after_attn = (tok_local.astype(jnp.float32) + attn_out).astype(jnp.bfloat16)
    gathered_mlp = lax.all_gather(after_attn, "gy", axis=1, tiled=True)
    normed_mlp = normalize(gathered_mlp, gain_mlp)
    feat_part = normed_mlp
    hidden_sum = jnp.dot(
        feat_part,
        lax.all_gather(w_up, "gx", axis=0, tiled=True),
        preferred_element_type=jnp.float32,
    )
    hidden = jax.nn.gelu(hidden_sum, approximate=False).astype(jnp.bfloat16)
    partials = jnp.dot(
        hidden, lax.all_gather(w_down, "gx", axis=1, tiled=True), preferred_element_type=jnp.float32
    )
    mlp_out = lax.psum_scatter(
        partials.astype(jnp.bfloat16), "gy", scatter_dimension=1, tiled=True
    ).astype(jnp.float32)
    after_mlp = (after_attn.astype(jnp.float32) + mlp_out).astype(jnp.bfloat16)
    picked = after_mlp[merge_groups[0]]
    merge_terms = jnp.einsum(
        "mkc,kcn->mn",
        picked,
        lax.all_gather(w_merge, "gx", axis=2, tiled=True),
        preferred_element_type=jnp.float32,
    )
    merged = lax.psum_scatter(
        merge_terms.astype(jnp.bfloat16), "gy", scatter_dimension=1, tiled=True
    )
    pooled = lax.all_gather(merged[None], "row", axis=0, tiled=True)
    stacked = pooled.reshape(-1, merged.shape[1])
    returned = stacked[sources[0]]
    return (after_mlp[None], returned[None])


def swap_x(arr):
    return lax.ppermute(arr, "gx", [(0, 1), (1, 0)])


def swap_y(arr):
    return lax.ppermute(arr, "gy", [(i, i ^ 2) for i in range(4)])


def swap_core(arr):
    return lax.ppermute(arr, "gy", [(i, i ^ 1) for i in range(4)])


def swap_row(arr, step):
    count = lax.axis_size("row")
    return lax.ppermute(arr, "row", [(i, i ^ step) for i in range(count)])


def gather_eight(own):
    over_x = swap_x(own)
    over_y = swap_y(own)
    held = [own, over_y, over_x, swap_y(over_x)]
    return held + [swap_core(part) for part in held]


PLACES = tuple((dx, dy, dc) for dc in (0, 1) for dx in (0, 1) for dy in (0, 1))


def position():
    gx = lax.axis_index("gx")
    gy = lax.axis_index("gy")
    return gx, gy // 2, gy % 2


def run_copies(pairs, sem):
    copies = [pltpu.make_async_copy(src, dst, sem.at[i]) for i, (src, dst) in enumerate(pairs)]
    for copy in copies:
        copy.start()
    return copies


def token_copies(refs, tok_scr):
    gx, y, core = position()
    width = refs[0].shape[0]
    pairs = []
    for ref, (dx, dy, dc) in zip(refs, PLACES):
        row = pl.multiple_of(((y ^ dy) * 2 + (core ^ dc)) * width, 16)
        pairs.append((ref, tok_scr.at[gx ^ dx, pl.ds(row, width)]))
    return pairs


STEP = 64


def column(row, scratch):
    scratch[...] = jnp.broadcast_to(row, (8, row.shape[1])).T


def side_by_side(pair, at):
    return jnp.concatenate([pair[0, at].astype(jnp.float32), pair[1, at].astype(jnp.float32)], axis=1)


def fold(rows):
    return jnp.sum(rows.reshape(rows.shape[0] // 8, 8, rows.shape[1]), axis=0)


def norm_of(pivot, first, second, feats):
    shift = jnp.sum(first, axis=0, keepdims=True) / feats
    variance = jnp.maximum(jnp.sum(second, axis=0, keepdims=True) / feats - shift * shift, 0.0)
    return pivot + shift, lax.rsqrt(variance + EPS)


def norm_tokens(pair, gain, out):
    _, feats, count = pair.shape
    steps = feats // STEP
    pivots = [pair[g, :16].astype(jnp.float32)[:1] for g in range(2)]

    def add_up(i, totals):
        at = pl.ds(pl.multiple_of(i * STEP, STEP), STEP)
        new = []
        for g in range(2):
            rows = pair[g, at].astype(jnp.float32) - pivots[g]
            new.append(totals[2 * g] + fold(rows))
            new.append(totals[2 * g + 1] + fold(rows * rows))
        return tuple(new)

    zero = jnp.zeros((8, count), jnp.float32)
    totals = lax.fori_loop(0, steps, add_up, (zero,) * 4)
    moments = [norm_of(pivots[g], totals[2 * g], totals[2 * g + 1], feats) for g in range(2)]
    mean, scale = (jnp.concatenate([moments[0][i], moments[1][i]], axis=1) for i in range(2))

    def write(i, carry):
        at = pl.ds(pl.multiple_of(i * STEP, STEP), STEP)
        rows = side_by_side(pair, at) - mean
        out[at, :] = (rows * scale * gain[at, :1]).astype(jnp.bfloat16)
        return carry

    lax.fori_loop(0, steps, write, 0)


def matmul(lhs, rhs):
    return jnp.dot(lhs, rhs, preferred_element_type=jnp.float32)


def dot_first(lhs, rhs):
    return lax.dot_general(lhs, rhs, (((0,), (0,)), ((), ())), preferred_element_type=jnp.float32)


def attention_kernel(*refs):
    shards = refs[:8]
    gain, w_query, w_key, w_value, w_got, w_got_row, w_got_key, segments = refs[8:16]
    out, tok_scr, norm_scr, w_scr, qkv_scr, att_scr, gain_scr, seg_scr, sem = refs[-9:]
    gx, y, core = position()
    plane = lax.axis_index("row") % 2
    cols = out.shape[0]
    pairs = token_copies(shards, tok_scr)
    own = pl.ds(pl.multiple_of(gx * cols, 16), cols)
    for i, ref in enumerate((w_query, w_key, w_value)):
        pairs.append((ref.at[own], w_scr.at[gx, pl.ds(i * cols, cols)]))
    pairs.append((w_got, w_scr.at[1 - gx, pl.ds(pl.multiple_of(2 * cols * plane, 16), cols)]))
    pairs.append((w_got_row, w_scr.at[1 - gx, pl.ds(pl.multiple_of(2 * cols * (1 - plane), 16), cols)]))
    pairs.append((w_got_key, w_scr.at[1 - gx, pl.ds(cols, cols)]))
    copies = run_copies(pairs, sem)
    column(gain[...], gain_scr)
    column(segments[...], seg_scr)
    for copy in copies[:8]:
        copy.wait()
    norm_tokens(tok_scr, gain_scr, norm_scr)
    for copy in copies[8:]:
        copy.wait()
    feats, total = norm_scr.shape
    depth = feats // 2
    qkv_scr[...] = matmul(w_scr[0], norm_scr[:depth]) + matmul(w_scr[1], norm_scr[depth:])
    scale = HD ** (-0.5) * LOG2_E
    for head in range(cols // HD):
        begin = head * HD
        keys = qkv_scr[cols + begin : cols + begin + HD].T.astype(jnp.bfloat16)
        values = qkv_scr[2 * cols + begin : 2 * cols + begin + HD].astype(jnp.bfloat16)
        for start in range(0, total, 256):
            at = slice(start, min(start + 256, total))
            scores = matmul(keys, (qkv_scr[begin : begin + HD, at] * scale).astype(jnp.bfloat16))
            scores = jnp.where(seg_scr[:, :1] == segments[:, at], scores, NEG)
            weights = jnp.exp2(scores - jnp.max(scores, axis=0, keepdims=True))
            row_total = jnp.sum(weights, axis=0, keepdims=True)
            att_scr[begin : begin + HD, at] = matmul(values, weights.astype(jnp.bfloat16)) / row_total
    out[...] = att_scr[...].astype(jnp.bfloat16)


def project_kernel(*refs):
    tokens, attended, weights, gain = refs[:8], refs[8:16], refs[16:20], refs[20]
    normed, own, tok_scr, att_scr, w_scr, aft_scr, gain_scr, sem = refs[-8:]
    gx, y, core = position()
    width = own.shape[0]
    cols = attended[0].shape[0]
    feats, total = att_scr.shape
    pairs = []
    for ref, (dx, dy, dc) in zip(attended, PLACES):
        row = pl.multiple_of(((y ^ dy) * 2 + (core ^ dc)) * width + (gx ^ dx) * cols, 16)
        pairs.append((ref, att_scr.at[pl.ds(row, cols)]))
    bounds = list(range(0, feats, 384))[:-1] + [feats]
    chunks = list(zip(bounds[:-1], bounds[1:]))
    for begin, end in chunks:
        for dc, parts in enumerate((weights[:2], weights[2:])):
            here = (y * 2 + (core ^ dc)) * width
            there = ((y ^ 1) * 2 + (core ^ dc)) * width
            for ref, row in zip(parts, (here, there)):
                at = pl.ds(pl.multiple_of(row, 16), ref.shape[0])
                pairs.append((ref.at[:, begin:end], w_scr.at[at, begin:end]))
        if begin == 0:
            pairs.extend(token_copies(tokens, tok_scr))
    copies = run_copies(pairs, sem)
    column(gain[...], gain_scr)
    first = second = pivot = None
    waited = 0
    for i, (begin, end) in enumerate(chunks):
        needed = 8 + 4 + 8 + 4 * i
        for copy in copies[waited:needed]:
            copy.wait()
        waited = needed
        rows = dot_first(w_scr[:, begin:end], att_scr[...]) + side_by_side(tok_scr, slice(begin, end))
        rows = rows.astype(jnp.bfloat16)
        aft_scr[begin:end] = rows
        rows = rows.astype(jnp.float32)
        if pivot is None:
            pivot = rows[:1]
        rows = rows - pivot
        sums = fold(rows), fold(rows * rows)
        first, second = sums if first is None else (first + sums[0], second + sums[1])
    mean, scale = norm_of(pivot, first, second, feats)
    row = pl.multiple_of((y * 2 + core) * width, 16)
    mine = aft_scr[pl.ds(row, width)].astype(jnp.float32)
    half = total // 2
    own[...] = jnp.where(gx == 0, mine[:, :half], mine[:, half:]).astype(jnp.bfloat16)

    def write(i, carry):
        at = pl.ds(pl.multiple_of(i * STEP, STEP), STEP)
        rows = aft_scr[at, :].astype(jnp.float32) - mean
        normed[at, :] = (rows * scale * gain_scr[at, :1]).astype(jnp.bfloat16)
        return carry

    lax.fori_loop(0, feats // STEP, write, 0)


def chunk_places(got, piece):
    plane = lax.axis_index("row") % 2
    for i, ref in enumerate(got):
        place = plane if i < 2 else 1 - plane
        yield ref, pl.ds(pl.multiple_of((2 * place + i % 2) * piece, 128), piece)


def up_kernel(normed, up_own, *refs):
    got, (hidden, norm_scr, up_scr, sem) = refs[:4], refs[4:]
    gx, y, core = position()
    feats, units = up_scr.shape
    depth = feats // 2
    own_rows = pl.ds(pl.multiple_of(gx * depth, 16), depth)
    other_rows = pl.ds(pl.multiple_of((1 - gx) * depth, 16), depth)
    pairs = [
        (normed, norm_scr),
        (up_own.at[:, pl.ds(pl.multiple_of(gx * units, 128), units)], up_scr.at[own_rows]),
    ]
    for ref, at in chunk_places(got, units // 4):
        pairs.append((ref, up_scr.at[other_rows, at]))
    for copy in run_copies(pairs, sem):
        copy.wait()
    for begin in range(0, units, 256):
        rows = dot_first(up_scr[:, begin : begin + 256], norm_scr[...])
        rows = 0.5 * rows * (1.0 + lax.erf(rows * (0.5**0.5)))
        hidden[begin : begin + 256] = rows.astype(jnp.bfloat16)


def down_kernel(dc, hidden, down_own, *refs):
    got, outs, (hid_scr, down_scr, sem) = refs[:4], refs[-7:-3], refs[-3:]
    gx, y, core = position()
    depth = down_own.shape[0]
    units, total = hid_scr.shape
    own_rows = pl.ds(pl.multiple_of(gx * depth, 16), depth)
    other_rows = pl.ds(pl.multiple_of((1 - gx) * depth, 16), depth)
    pairs = [
        (hidden, hid_scr),
        (down_own.at[:, pl.ds(pl.multiple_of(gx * units, 128), units)], down_scr.at[own_rows]),
    ]
    for ref, at in chunk_places(got, units // 4):
        pairs.append((ref, down_scr.at[other_rows, at]))
    for copy in run_copies(pairs, sem):
        copy.wait()
    half = outs[0].shape[1]
    middle = total // 2
    for dy in range(2):
        for part in range(2):
            row = ((y ^ dy) * 2 + (core ^ dc)) * (2 * half) + part * half
            sums = matmul(down_scr[pl.ds(pl.multiple_of(row, 16), half)], hid_scr[...])
            left, right = sums[:, :middle], sums[:, middle:]
            for dx in range(2):
                group, other = (dx, dy) if part == 0 else (dy, dx)
                picked = jnp.where(gx == dx, left, right)
                outs[2 * (1 - group) + part][other] = picked.astype(jnp.bfloat16)


def last_sum_kernel(own, rest_x, rest_y, last_x, last_y, groups, out, picked):
    half, count = last_x.shape
    for i, (rest, source) in enumerate(((rest_x, last_x), (rest_y, last_y))):
        at = slice(i * half, (i + 1) * half)
        total = own[at].astype(jnp.float32) + rest[...].astype(jnp.float32) + source[...].astype(jnp.float32)
        out[at] = total.astype(jnp.bfloat16)
    for k in range(groups.shape[0]):
        place = lax.broadcasted_iota(jnp.int32, (count, groups.shape[1]), 0)
        chosen = jnp.where(place == groups[k : k + 1], 1.0, 0.0).astype(jnp.bfloat16)
        picked[k] = matmul(out[...], chosen).T.astype(jnp.bfloat16)


def merge_kernel(picked, weights, *refs):
    got, (keep, send, res_scr) = refs[:4], refs[-3:]
    gx, y, core = position()
    plane = lax.axis_index("row") % 2
    slots = weights.shape[0]
    width = keep.shape[1]
    own = matmul(picked[0], weights[0])
    for k in range(1, slots):
        own = own + matmul(picked[k], weights[k])
    other = None
    for i, ref in enumerate(got):
        place = plane if i < 2 else 1 - plane
        part = matmul(picked[2 * place + i % 2], ref[...])
        other = part if other is None else other + part
    res_scr[gx] = own.T
    res_scr[1 - gx] = other.T
    for dc, target in ((0, keep), (1, send)):
        row = pl.multiple_of((core ^ dc) * width, 16)
        for dy in range(2):
            target[dy] = res_scr[y ^ dy, pl.ds(row, width)].astype(jnp.bfloat16)


def add(*arrs):
    total = arrs[0].astype(jnp.float32)
    for arr in arrs[1:]:
        total = total + arr.astype(jnp.float32)
    return total.astype(jnp.bfloat16)


def return_kernel(*refs):
    tiles, sources, out = refs[:-2], refs[-2], refs[-1]
    row = lax.axis_index("row")
    count = sources.shape[1]
    total = None
    for step, tile in enumerate(tiles):
        slot = lax.broadcasted_iota(jnp.int32, (tile.shape[1], count), 0) + (row ^ step) * tile.shape[1]
        chosen = jnp.where(slot == sources[...], 1.0, 0.0).astype(jnp.bfloat16)
        part = matmul(tile[...], chosen)
        total = part if total is None else total + part
    out[...] = total.astype(jnp.bfloat16)


def call(kernel, operands, outs, far, scratch=(), flops=0, aliases=None, far_out=False, limit=VMEM_LIMIT):
    moved = sum(a.size * a.dtype.itemsize for a in operands)
    outs = tuple(jax.ShapeDtypeStruct(shape, dtype) for shape, dtype in outs)
    return pl.pallas_call(
        kernel,
        out_shape=outs,
        in_specs=[pl.BlockSpec(memory_space=pl.ANY if f else pltpu.VMEM) for f in far],
        out_specs=tuple(pl.BlockSpec(memory_space=pl.ANY if far_out else pltpu.VMEM) for _ in outs),
        scratch_shapes=list(scratch),
        input_output_aliases=aliases or {},
        compiler_params=pltpu.CompilerParams(vmem_limit_bytes=limit),
        cost_estimate=pl.CostEstimate(flops=flops, bytes_accessed=moved, transcendentals=0),
    )(*operands)


def after(held, passed):
    count = len(passed)
    return call(
        lambda *refs: None,
        (*passed, *held),
        [(a.shape, a.dtype) for a in passed],
        (True,) * (count + len(held)),
        aliases={i: i for i in range(count)},
        far_out=True,
    )


def rows_of(arr, begin, count):
    return lax.dynamic_slice_in_dim(arr, begin, count, 0)


def fast_body(
    tokens,
    segments,
    gain_attn,
    w_query,
    w_key,
    w_value,
    w_out,
    gain_mlp,
    w_up,
    w_down,
    w_merge,
    merge_groups,
    sources,
):
    gx = lax.axis_index("gx")
    plane = lax.axis_index("row") % 2
    tok = tokens[0].T
    width, count = tok.shape
    feats = 4 * width
    depth = feats // 2
    half = width // 2
    cols = w_query.shape[1] // 2
    total_cols = 3 * cols
    sixteen = jnp.bfloat16
    total = 2 * count
    gain_attn = gain_attn.reshape(1, -1)
    gain_mlp = gain_mlp.reshape(1, -1)
    down = w_down.T
    units = w_up.shape[1] // 2
    chunk = units // 2
    theirs = (1 - gx) * units + plane * chunk
    their_row = (1 - gx) * cols
    first = jnp.where(
        plane == 0, rows_of(w_query.T, their_row, cols), rows_of(w_value.T, their_row, cols)
    )

    over_x, over_y = swap_x(tok), swap_y(tok)
    qkv_got = swap_x(first)
    (key_piece,) = after((qkv_got, over_y), (rows_of(w_key.T, their_row, cols),))
    qkv_got_key = swap_x(key_piece)
    held = [tok, over_y, over_x, swap_y(over_x)]
    tok_shards = held + [swap_core(part) for part in held]
    piece = chunk // 2
    down_a, down_b = (lax.dynamic_slice_in_dim(down, theirs + i * piece, piece, 1) for i in range(2))
    up_a, up_b = (lax.dynamic_slice_in_dim(w_up, theirs + i * piece, piece, 1) for i in range(2))
    (up_a,) = after((qkv_got, over_x), (up_a,))
    up_got_a = swap_x(up_a)
    qkv_got_row = swap_row(qkv_got, 1)
    (out_piece,) = after((held[3],), (w_out,))
    out_over_y = [swap_y(out_piece)]
    up_b, down_a, down_b = after(
        (qkv_got_row, qkv_got_key, held[3], *tok_shards[4:7], out_piece), (up_b, down_a, down_b)
    )
    up_got_b, down_got_a = swap_x(up_b), swap_x(down_a)
    up_got_a_row = swap_row(up_got_a, 1)

    (attended,) = call(
        attention_kernel,
        (*tok_shards, gain_attn, w_query.T, w_key.T, w_value.T, qkv_got, qkv_got_row, qkv_got_key, segments, up_got_a),
        [((cols, total), sixteen)],
        (True,) * 8 + (False,) + (True,) * 6 + (False, True),
        [
            pltpu.VMEM((2, feats, count), sixteen),
            pltpu.VMEM((feats, total), sixteen),
            pltpu.VMEM((2, total_cols, depth), sixteen),
            pltpu.VMEM((total_cols, total), jnp.float32),
            pltpu.VMEM((cols, total), jnp.float32),
            pltpu.VMEM((feats, 8), jnp.float32),
            pltpu.VMEM((total, 8), jnp.int32),
            pltpu.SemaphoreType.DMA((14,)),
        ],
        2 * total * feats * total_cols + 4 * total * total * cols,
    )
    attended, up_got_b, down_got_a = after((up_got_a_row,), (attended, up_got_b, down_got_a))
    over_x, over_y = swap_x(attended), swap_y(attended)
    up_got_b_row, down_got_a_row = swap_row(up_got_b, 1), swap_row(down_got_a, 1)
    slots = w_merge.shape[0]
    merge_pieces = [rows_of(w_merge, plane * (slots // 2) + i, 1)[0] for i in range(2)]
    *out_over_y, down_b = after((over_x, over_y, up_got_b_row), (*out_over_y, down_b))
    down_got_b = swap_x(down_b)
    diagonal, *merge_pieces = after((down_got_a_row, down_got_b), (swap_y(over_x), *merge_pieces))
    held = [attended, over_y, over_x, diagonal]
    att_shards = held + [swap_core(part) for part in held]
    out_parts = [w_out, *out_over_y]
    out_parts = out_parts + [swap_core(part) for part in out_parts]
    down_got_b_row = swap_row(down_got_b, 1)
    normed, own = call(
        project_kernel,
        (*tok_shards, *att_shards, *out_parts, gain_mlp, down_got_b, down_got_a_row),
        [((feats, total), sixteen), ((width, count), sixteen)],
        (True,) * 20 + (False, True, True),
        [
            pltpu.VMEM((2, feats, count), sixteen),
            pltpu.VMEM((feats, total), sixteen),
            pltpu.VMEM((feats, feats), sixteen),
            pltpu.VMEM((feats, total), sixteen),
            pltpu.VMEM((feats, 8), jnp.float32),
            pltpu.SemaphoreType.DMA((32,)),
        ],
        2 * total * feats * feats,
    )
    merge_got = [swap_x(part) for part in merge_pieces]
    normed, merge_got[0] = after((), (normed, merge_got[0]))
    (hidden,) = call(
        up_kernel,
        (normed, w_up, up_got_a, up_got_b, up_got_a_row, up_got_b_row),
        [((units, total), sixteen)],
        (True,) * 6,
        [
            pltpu.VMEM((feats, total), sixteen),
            pltpu.VMEM((feats, units), sixteen),
            pltpu.SemaphoreType.DMA((6,)),
        ],
        2 * total * feats * units,
        limit=SMALL_LIMIT,
    )
    pair = ((2, half, count), sixteen)

    def down_part(dc, *others):
        return call(
            functools.partial(down_kernel, dc),
            (hidden, down, down_got_a, down_got_b, down_got_a_row, down_got_b_row, *others),
            [pair] * 4,
            (True,) * (6 + len(others)),
            [
                pltpu.VMEM((units, total), sixteen),
                pltpu.VMEM((feats, units), sixteen),
                pltpu.SemaphoreType.DMA((6,)),
            ],
            total * feats * units,
            limit=SMALL_LIMIT,
        )

    send = down_part(1)
    got = [swap_core(part) for part in send]
    merge_got_row = [swap_row(part, 1) for part in merge_got]
    keep = down_part(0, *send)
    keep = after((merge_got[1], merge_got_row[0]), keep)
    from_x = swap_x(add(keep[0], got[0]))
    from_y = swap_y(add(keep[1], got[1]))
    rest_x, rest_y = add(keep[2], got[2], from_x), add(keep[3], got[3], from_y)
    last_x, last_y = swap_y(rest_x[1]), swap_x(rest_y[1])
    merged_count = merge_groups.shape[1]
    after_mlp, picked = call(
        last_sum_kernel,
        (own, rest_x[0], rest_y[0], last_x, last_y, merge_groups[0].T),
        [((width, count), sixteen), ((slots, merged_count, width), sixteen)],
        (False,) * 6,
        (),
        2 * count * width * count,
        limit=SMALL_LIMIT,
    )
    keep, send = call(
        merge_kernel,
        (picked, w_merge, *merge_got, *merge_got_row),
        [((2, width, merged_count), sixteen)] * 2,
        (False,) * 6,
        [pltpu.VMEM((2, depth, merged_count), jnp.float32)],
        2 * count * width * feats,
        limit=SMALL_LIMIT,
    )
    mine = add(keep, swap_core(send))
    merged = add(mine[0], swap_y(mine[1]))
    tiles = [merged] + [swap_row(merged, step) for step in range(1, lax.axis_size("row"))]
    (returned,) = call(
        return_kernel,
        (*tiles, sources),
        [((width, merged_count), sixteen)],
        (False,) * (len(tiles) + 1),
        (),
        2 * count * width * merged_count,
        limit=SMALL_LIMIT,
    )
    return (after_mlp.T[None], returned.T[None])


def solution(mesh):
    placed = (
        P("row", "gx", "gy"),
        P("row", None),
        P(),
        P("gx", "gy"),
        P("gx", "gy"),
        P("gx", "gy"),
        P("gy", None),
        P(),
        P("gx", "gy"),
        P("gy", "gx"),
        P(None, "gy", "gx"),
        P("row", "gx", None),
        P("row", "gx"),
    )
    small = mesh.shape["gx"] == 2 and mesh.shape["gy"] == 4 and mesh.shape["row"] in (2, 4)
    return jax.shard_map(
        fast_body if small else general_body,
        mesh=mesh,
        in_specs=placed,
        out_specs=(P("row", "gx", "gy"), P("row", "gx", "gy")),
        check_vma=False,
    )
```
